128 devices in a mesh: group: 8 (over x, core), dom: 16 (over y, z).
Axes of the slice: x: 4, y: 4, z: 4, core: 2. Of those that a mesh axis runs over, the one named last changes fastest.
Arguments:
- features: bfloat16 [65536, 512], P(('group', 'dom')), may hold values from -6 to 6
- w_query: bfloat16 [512, 512], replicated
- w_key: bfloat16 [512, 512], replicated
- w_value: bfloat16 [512, 512], replicated, may hold values from -0.25 to 0.25
- w_out: bfloat16 [512, 512], replicated, may hold values from -0.25 to 0.25
- w_up: bfloat16 [512, 2048], replicated, may hold values from -0.25 to 0.25
- w_down: bfloat16 [2048, 512], replicated, may hold values from -0.125 to 0.125
- block_len: int32 [512], P(('group', 'dom')), may hold values from 32 to 128, as said below
- cross_blocks: int32 [512, 2], P(('group', 'dom')), may hold values from 0 to 511, as said below
- cross_count: int32 [512], P(('group', 'dom')), may hold values from 1 to 2, as said below
Outputs:
- layer_out: bfloat16 [65536, 512], P(('group', 'dom'))
The draws below stay inside these ranges and needn't reach their ends.
Inputs may be any that keep to these rules, and one draw needn't show every extreme that they name: `block_len`: block 0 has all 128 nodes live. Block cross_blocks[b, c] lies in a group other than b's, at the same index of dom as block b, that is cross_blocks[b, c] // 4 % 16 == b // 4 % 16. `cross_count`: block 0 uses all 2 listed key blocks.
All inputs are finite; a program needn't handle non-finite values.
Results may differ from the reference program's by a relative error of at most 0.012.
The reference program's roundings to bfloat16 on the way count: a program that leaves them out, or rounds other values in their place, can miss the bound.
Values may be sent and summed in bfloat16 or wider, within the bound.
A program may use at most 320 MiB of HBM per device.

```python
import jax
import jax.numpy as jnp
from jax import lax

D = 512
HEADS = 8
FF = 2048
BLK = 128
CROSS = 2
NB_DEV = 4
TOK_DEV = 512
NBLK = 512
NODES = 65536
N_GROUP = 8
N_DOM = 16


def projection_pair(key):
    base = jax.random.fold_in(key, 7)
    first = jax.random.normal(jax.random.fold_in(base, 1), (D, D), jnp.float32)
    second = jax.random.normal(jax.random.fold_in(base, 2), (D, D), jnp.float32)
    w_first = first * (3.0 / D ** 0.5)
    w_second = second * (1.0 / D ** 0.5)
    return (w_first, w_second)


def draw_w_query(key, part):
    return projection_pair(key)[0].astype(jnp.bfloat16)


def draw_w_key(key, part):
    return projection_pair(key)[1].astype(jnp.bfloat16)


def draw_block_len(key, part):
    lengths = jax.random.randint(jax.random.fold_in(key, 11), (NBLK,), BLK // 4, BLK + 1, jnp.int32)
    return lengths.at[0].set(BLK)


def draw_cross_blocks(key, part):
    block_ids = jnp.arange(NBLK, dtype=jnp.int32)
    group_ids = block_ids // (N_DOM * NB_DEV)
    dom_ids = block_ids // NB_DEV % N_DOM
    offsets = jax.random.randint(jax.random.fold_in(key, 21), (NBLK, CROSS), 1, N_GROUP, jnp.int32)
    locals_drawn = jax.random.randint(jax.random.fold_in(key, 22), (NBLK, CROSS), 0, NB_DEV, jnp.int32)
    other = (group_ids[:, None] + offsets) % N_GROUP
    return ((other * N_DOM + dom_ids[:, None]) * NB_DEV + locals_drawn).astype(jnp.int32)


def draw_cross_count(key, part):
    counts = jax.random.randint(jax.random.fold_in(key, 31), (NBLK,), 1, CROSS + 1, jnp.int32)
    return counts.at[0].set(CROSS)


def level_of(key, dims, pieces, smallest, high):
    factor_of, own = 1.0, jax.random.fold_in(key, 6)
    for position, parts in pieces:
        draws = jnp.exp(jax.random.uniform(jax.random.fold_in(own, position), (parts,), jnp.float32, smallest / len(pieces), high / len(pieces)))
        factor_of = factor_of * jnp.repeat(draws, dims[position] // parts).reshape([-1 if axis == position else 1 for axis in range(len(dims))])
    return factor_of


def normal_values(key, dims, width, reach, cuts=(), held_as=jnp.bfloat16):
    drawn = width * jax.random.normal(key, dims, jnp.float32)
    if cuts:
        drawn = drawn * level_of(key, dims, cuts, -0.22, 0.18)
    return jnp.clip(drawn, -reach, reach).astype(held_as)


def setup_inputs(seed: int = 0) -> dict:
    splits = jax.random.split(jax.random.key(seed), 11)
    features = normal_values(splits[0], (NODES, D), 1.0, 6.0, ((0, 128),))
    w_query = draw_w_query(jax.random.fold_in(splits[10], 71), 0)
    w_key = draw_w_key(jax.random.fold_in(splits[10], 71), 0)
    w_value = normal_values(splits[3], (D, D), D ** -0.5, 0.25)
    w_out = normal_values(splits[4], (D, D), D ** -0.5, 0.25)
    w_up = normal_values(splits[5], (D, FF), D ** -0.5, 0.25)
    w_down = normal_values(splits[6], (FF, D), FF ** -0.5, 0.125)
    block_len = draw_block_len(jax.random.fold_in(splits[10], 71), 0)
    cross_blocks = draw_cross_blocks(jax.random.fold_in(splits[10], 71), 0)
    cross_count = draw_cross_count(jax.random.fold_in(splits[10], 71), 0)
    return {"features": features, "w_query": w_query, "w_key": w_key, "w_value": w_value, "w_out": w_out, "w_up": w_up, "w_down": w_down, "block_len": block_len, "cross_blocks": cross_blocks, "cross_count": cross_count}


def rms_normed(values):
    wide = values.astype(jnp.float32)
    return (wide * lax.rsqrt(lax.optimization_barrier(jnp.mean(wide * wide, axis=-1, keepdims=True)) + 1e-06)).astype(jnp.bfloat16)

def attend(query_rows, key_rows, value_rows, live_mask):
    count_q = query_rows.shape[0]
    count_k = key_rows.shape[0]
    q_heads = query_rows.reshape(count_q, HEADS, -1).astype(jnp.float32)
    k_heads = key_rows.reshape(count_k, HEADS, -1).astype(jnp.float32)
    v_heads = value_rows.reshape(count_k, HEADS, -1).astype(jnp.float32)
    scale = 1.0 / q_heads.shape[-1] ** 0.5
    scores = jnp.einsum('rhd,shd->hrs', q_heads, k_heads) * scale
    scores = jnp.where(live_mask[None, None, :], scores, -1e+30)
    top = lax.optimization_barrier(jnp.max(scores, axis=-1, keepdims=True))
    weights = jnp.where(live_mask[None, None, :], jnp.exp(scores - top), 0.0)
    total = lax.optimization_barrier(jnp.sum(weights, axis=-1))
    rounded = lax.optimization_barrier(weights.astype(jnp.bfloat16)).astype(jnp.float32)
    summed = jnp.einsum('hrs,shd->rhd', rounded, v_heads)
    return (summed / jnp.transpose(total)[:, :, None]).reshape(count_q, -1)

def reference(features, w_query, w_key, w_value, w_out, w_up, w_down, block_len, cross_blocks, cross_count):
    nodes = features.shape[0]
    blocks = nodes // BLK
    live_blocks = jnp.arange(BLK, dtype=jnp.int32)[None, :] < block_len[:, None]
    live = live_blocks.reshape(nodes)
    normed = rms_normed(features)
    query = jnp.dot(normed, w_query, preferred_element_type=jnp.float32).astype(jnp.bfloat16)
    keys = jnp.dot(normed, w_key, preferred_element_type=jnp.float32).astype(jnp.bfloat16)
    values = jnp.dot(normed, w_value, preferred_element_type=jnp.float32).astype(jnp.bfloat16)
    group_nodes = TOK_DEV * N_DOM
    span_count = nodes // TOK_DEV

    def intra_span(index):
        start = (index * TOK_DEV).astype(jnp.int32)
        group_start = (index // N_DOM * group_nodes).astype(jnp.int32)
        q_rows = lax.dynamic_slice_in_dim(query, start, TOK_DEV, 0)
        k_rows = lax.dynamic_slice_in_dim(keys, group_start, group_nodes, 0)
        v_rows = lax.dynamic_slice_in_dim(values, group_start, group_nodes, 0)
        m_rows = lax.dynamic_slice_in_dim(live, group_start, group_nodes, 0)
        return attend(q_rows, k_rows, v_rows, m_rows)
    intra = lax.map(intra_span, jnp.arange(span_count, dtype=jnp.int32)).reshape(nodes, -1)
    key_blocks = keys.reshape(blocks, BLK, -1)
    value_blocks = values.reshape(blocks, BLK, -1)
    query_blocks = query.reshape(blocks, BLK, -1)

    def cross_block(index):
        chosen = cross_blocks[index]
        k_rows = key_blocks[chosen].reshape(CROSS * BLK, -1)
        v_rows = value_blocks[chosen].reshape(CROSS * BLK, -1)
        used = jnp.arange(CROSS, dtype=jnp.int32) < cross_count[index]
        m_rows = (live_blocks[chosen] & used[:, None]).reshape(CROSS * BLK)
        return attend(query_blocks[index], k_rows, v_rows, m_rows)
    cross = lax.map(cross_block, jnp.arange(blocks, dtype=jnp.int32)).reshape(nodes, -1)
    mixed = (intra + cross).astype(jnp.bfloat16)
    resid = (features.astype(jnp.float32) + jnp.dot(mixed, w_out, preferred_element_type=jnp.float32)).astype(jnp.bfloat16)
    normed_two = rms_normed(resid)
    hidden = jax.nn.gelu(jnp.dot(normed_two, w_up, preferred_element_type=jnp.float32)).astype(jnp.bfloat16)
    return (resid.astype(jnp.float32) + jnp.dot(hidden, w_down, preferred_element_type=jnp.float32)).astype(jnp.bfloat16)
```

```python
import functools
import math

import jax
import jax.numpy as jnp
from jax import lax
from jax.experimental import pallas as pl
from jax.experimental.pallas import tpu as pltpu
from jax.sharding import PartitionSpec as P

F32, BF16 = jnp.float32, jnp.bfloat16
MESH = pl.DeviceIdType.MESH
HEADS = 8
HEAD = 64
BLK = 128
TOK = 512
D = 512
FF = 2048
VROWS = 80
ROUNDS = 16
NEG = -1e30
FLAG = 64.0
SOURCE = (
    (0, 0), (0, 1), (1, 0), (1, 1), (3, 0), (2, 0), (3, 1), (4, 0),
    (5, 1), (6, 0), (7, 0), (8, 0), (9, 0), (11, 0), (13, 0),
)


def dot(a, b):
    return jnp.dot(a, b, preferred_element_type=F32)


def dot_t(a, b):
    return lax.dot_general(a, b, (((1,), (1,)), ((), ())), preferred_element_type=F32)


def rms(wide):
    return (wide * lax.rsqrt(jnp.mean(wide * wide, axis=-1, keepdims=True) + 1e-06)).astype(BF16)


def kernel(
    len_ref, blocks_ref, count_ref, x_ref, wq_hbm, wk_hbm, wv_hbm, wo_hbm, wup_hbm, wdown_hbm,
    out_ref,
    wq, wk, wv, wo, wup, wdown, wvt, nrm, own, rbuf, xbuf, qt, ks, vt, acc, top, st, mix, w_sem,
    s_sem, r_sem, xs_sem, xr_sem, bs_sem, br_sem,
):
    weights = [(wq_hbm, wq), (wk_hbm, wk), (wv_hbm, wv), (wo_hbm, wo), (wup_hbm, wup), (wdown_hbm, wdown)]

    def fetch(k):
        return pltpu.make_async_copy(weights[k][0], weights[k][1], w_sem.at[k])

    for k in range(6):
        fetch(k).start()

    g, d = lax.axis_index("group"), lax.axis_index("dom")
    y, z = d // 4, d % 4
    up_y, dn_y = (y + 1) % 4 * 4 + z, (y + 3) % 4 * 4 + z
    up_z, dn_z = y * 4 + (z + 1) % 4, y * 4 + (z + 3) % 4
    towards = [(g, up_y), (g, up_z), (g, dn_y), (g, dn_z)]
    up_x, dn_x, sibling = ((g + 2) % 8, d), ((g + 6) % 8, d), (g + 1 - 2 * (g % 2), d)

    barrier = pltpu.get_barrier_semaphore()
    for other in [*towards, up_x, dn_x, sibling]:
        pl.semaphore_signal(barrier, inc=1, device_id=other, device_id_type=MESH)

    normed = rms(x_ref[...].astype(F32))
    nrm[...] = normed
    row = lax.broadcasted_iota(jnp.int32, (BLK, D), 0)
    lane = lax.broadcasted_iota(jnp.int32, (BLK, D), 1)
    flag = jnp.where((lane == 0) | (lane == 64), FLAG, 0.0)
    for b in range(4):
        part = normed[b * BLK:(b + 1) * BLK].astype(F32)
        flagged = jnp.where(row < len_ref[b], part, flag).astype(BF16)
        rbuf[0, b * BLK:(b + 1) * BLK, :] = flagged
        own[b] = flagged

    pl.semaphore_wait(barrier, 7)

    def send(n, link):
        slot, partner = SOURCE[n]
        return pltpu.make_async_remote_copy(
            src_ref=rbuf.at[slot, pl.ds((link ^ partner) * BLK, BLK)],
            dst_ref=rbuf.at[n + 1, pl.ds(link * BLK, BLK)],
            send_sem=s_sem.at[n, link], recv_sem=r_sem.at[n, link],
            device_id=towards[link], device_id_type=MESH,
        )

    def send_x(s, way):
        blocks = pl.ds(4 * s + 2 * way, 2)
        return pltpu.make_async_remote_copy(
            src_ref=own.at[pl.ds(2 * way, 2)] if s == 0 else xbuf.at[blocks],
            dst_ref=xbuf.at[pl.ds(4 * s + 4 + 2 * way, 2)],
            send_sem=xs_sem.at[s, way], recv_sem=xr_sem.at[s, way],
            device_id=(up_x, dn_x)[way], device_id_type=MESH,
        )

    def send_sibling(s):
        return pltpu.make_async_remote_copy(
            src_ref=own if s == 0 else xbuf.at[pl.ds(4 * s, 4)],
            dst_ref=xbuf.at[pl.ds(16 + 4 * s, 4)],
            send_sem=bs_sem.at[s], recv_sem=br_sem.at[s],
            device_id=sibling, device_id_type=MESH,
        )

    for n in range(2):
        for link in range(4):
            send(n, link).start()
    for way in range(2):
        send_x(0, way).start()
    send_sibling(0).start()

    fetch(0).wait()
    q_all = dot_t(jnp.transpose(wq[...].astype(F32)).astype(BF16), nrm[...]) * (math.log2(math.e) / 8.0)
    q_all = q_all.astype(BF16)
    ones = jnp.ones((HEAD, TOK), BF16)
    for h in range(HEADS):
        at = (h % 2) * HEAD
        qt[h, at:at + HEAD, :] = q_all[h * HEAD:(h + 1) * HEAD]
        qt[h, HEAD - at:HEAD - at + HEAD, :] = ones
        vt[h, HEAD:VROWS, :] = jnp.ones((VROWS - HEAD, TOK), BF16)
    fetch(1).wait()
    fetch(2).wait()
    wvt[...] = jnp.transpose(wv[...].astype(F32)).astype(BF16)
    acc[...] = jnp.zeros_like(acc)
    top[...] = jnp.full_like(top, NEG)

    def keys_of(rows, unused=None):
        n = rows.shape[0]
        ks[0:n, :] = dot(rows, wk[...]).astype(BF16)
        values = dot_t(wvt[...], rows).astype(BF16)
        for h in range(HEADS):
            vt[h, 0:HEAD, 0:n] = values[h * HEAD:(h + 1) * HEAD]
        mask = jnp.where(rows[:, 0:BLK].astype(F32) > FLAG / 2, NEG, 0.0)
        if unused is not None:
            mask = jnp.where(unused, NEG, mask)
        return mask.astype(BF16)

    def scores(h, n, mask, q):
        lane = lax.broadcasted_iota(jnp.int32, (n, BLK), 1)
        pair = ks[0:n, (h // 2) * BLK:(h // 2 + 1) * BLK]
        mine = (lane < HEAD) if h % 2 == 0 else (lane >= HEAD)
        return dot(jnp.where(mine, pair, mask), q)

    def attend(rows):
        mask = keys_of(rows)
        st[0] = scores(0, TOK, mask, qt[0])
        for h in range(HEADS):
            if h + 1 < HEADS:
                st[(h + 1) % 2] = scores(h + 1, TOK, mask, qt[h + 1])
            s = st[h % 2]
            old = top[h]
            new = jnp.maximum(old, jnp.max(s, axis=0, keepdims=True))
            top[h] = new
            p = jnp.exp2(s - new).astype(BF16)
            acc[h] = acc[h] * jnp.exp2(old - new) + dot(vt[h], p)

    def cross(b):
        picked = []
        for c in range(2):
            block = blocks_ref[b, c]
            group, local = lax.div(block, 64), lax.rem(block, 4)
            apart = (lax.div(g, 2) - lax.div(group, 2)) * (1 - 2 * lax.div(local, 2))
            slot = lax.rem(group + g, 2) * 16 + lax.rem(apart + 4, 4) * 4 + local
            picked.append(xbuf[slot])
        rows = jnp.concatenate(picked, axis=0)
        at = lax.broadcasted_iota(jnp.int32, (2 * BLK, BLK), 0) // BLK
        mask = keys_of(rows, at >= count_ref[b])
        here = pl.ds(b * BLK, BLK)
        for h in range(HEADS):
            s = scores(h, 2 * BLK, mask, qt[h, :, here])
            p = jnp.exp2(s - jnp.max(s, axis=0, keepdims=True)).astype(BF16)
            o = dot(vt[h, :, 0:2 * BLK], p)
            mix[h * HEAD:(h + 1) * HEAD, here] = o[0:HEAD] / o[HEAD:HEAD + 1]

    def round_(r, carry):
        for n in range(ROUNDS - 1):
            @pl.when(r == n + 1)
            def _(n=n):
                for link in range(4):
                    send(n, link).wait_recv()
                if n + 2 < ROUNDS - 1:
                    for link in range(4):
                        send(n + 2, link).start()
        for s in range(1, 4):
            @pl.when(r == 1 + 2 * s)
            def _(s=s):
                for way in range(2):
                    send_x(s - 1, way).wait_recv()
                    if s < 3:
                        send_x(s, way).start()
                send_sibling(s).start()
        attend(rbuf[r])
        return carry

    lax.fori_loop(0, ROUNDS, round_, 0)

    for s in range(4):
        send_sibling(s).wait_recv()
    for b in range(4):
        cross(b)

    for n in range(ROUNDS - 1):
        for link in range(4):
            send(n, link).wait_send()
    for s in range(3):
        for way in range(2):
            send_x(s, way).wait_send()
    for s in range(4):
        send_sibling(s).wait_send()

    for h in range(HEADS):
        at = slice(h * HEAD, (h + 1) * HEAD)
        mix[at, :] = mix[at, :] + acc[h, 0:HEAD] / acc[h, HEAD:HEAD + 1]
    mixed = jnp.transpose(mix[...]).astype(BF16)
    for k in range(3, 6):
        fetch(k).wait()
    resid = (x_ref[...].astype(F32) + dot(mixed, wo[...])).astype(BF16)
    normed_two = rms(resid.astype(F32))
    total = resid.astype(F32)
    for k in range(FF // TOK):
        cols = slice(k * TOK, (k + 1) * TOK)
        hidden = jax.nn.gelu(dot(normed_two, wup[:, cols])).astype(BF16)
        total = total + dot(hidden, wdown[cols, :])
    out_ref[...] = total.astype(BF16)


def body(features, w_query, w_key, w_value, w_out, w_up, w_down, block_len, cross_blocks, cross_count):
    smem = pl.BlockSpec(memory_space=pltpu.SMEM)
    vmem = pl.BlockSpec(memory_space=pltpu.VMEM)
    hbm = pl.BlockSpec(memory_space=pl.ANY)
    dma = pltpu.SemaphoreType.DMA
    return pl.pallas_call(
        kernel,
        out_shape=jax.ShapeDtypeStruct((TOK, D), BF16),
        in_specs=[smem] * 3 + [vmem] + [hbm] * 6,
        out_specs=vmem,
        scratch_shapes=[
            pltpu.VMEM((D, D), BF16), pltpu.VMEM((D, D), BF16), pltpu.VMEM((D, D), BF16), pltpu.VMEM((D, D), BF16),
            pltpu.VMEM((D, FF), BF16), pltpu.VMEM((FF, D), BF16),
            pltpu.VMEM((D, D), BF16),
            pltpu.VMEM((TOK, D), BF16),
            pltpu.VMEM((4, BLK, D), BF16),
            pltpu.VMEM((ROUNDS, TOK, D), BF16),
            pltpu.VMEM((32, BLK, D), BF16),
            pltpu.VMEM((HEADS, 2 * HEAD, TOK), BF16),
            pltpu.VMEM((TOK, D), BF16),
            pltpu.VMEM((HEADS, VROWS, TOK), BF16),
            pltpu.VMEM((HEADS, VROWS, TOK), F32),
            pltpu.VMEM((HEADS, 1, TOK), F32),
            pltpu.VMEM((2, TOK, TOK), F32),
            pltpu.VMEM((D, TOK), F32),
            dma((6,)),
            dma((ROUNDS - 1, 4)), dma((ROUNDS - 1, 4)),
            dma((3, 2)), dma((3, 2)), dma((4,)), dma((4,)),
        ],
        compiler_params=pltpu.CompilerParams(
            collective_id=0, has_side_effects=True, vmem_limit_bytes=60 * 2**20
        ),
        name="layer",
    )(block_len, cross_blocks, cross_count, features, w_query, w_key, w_value, w_out, w_up, w_down)


def solution(mesh):
    both = P(("group", "dom"))
    rows = P(("group", "dom"), None)
    return jax.shard_map(
        body,
        mesh=mesh,
        in_specs=(rows, P(), P(), P(), P(), P(), P(), both, rows, both),
        out_specs=rows,
        check_vma=False,
    )
```

```python
import functools
import math

import jax
import jax.numpy as jnp
from jax import lax
from jax.experimental import pallas as pl
from jax.experimental.pallas import tpu as pltpu
from jax.sharding import PartitionSpec as P

F32, BF16 = jnp.float32, jnp.bfloat16
MESH = pl.DeviceIdType.MESH
HEADS = 8
HEAD = 64
BLK = 128
TOK = 512
D = 512
FF = 2048
VROWS = 80
ROUNDS = 16
NEG = -1e30
FLAG = 64.0
SOURCE = (
    (-1, 0), (-1, 2), (-1, 1), (-1, 3), (0, 0), (0, 1), (0, 3), (1, 3),
    (1, 1), (2, 0), (4, 1), (4, 3), (5, 0), (7, 0), (10, 0),
)


def dot(a, b):
    return jnp.dot(a, b, preferred_element_type=F32)


def dot_t(a, b):
    return lax.dot_general(a, b, (((1,), (1,)), ((), ())), preferred_element_type=F32)


def rms(wide):
    return (wide * lax.rsqrt(jnp.mean(wide * wide, axis=-1, keepdims=True) + 1e-06)).astype(BF16)


def kernel(
    len_ref, blocks_ref, count_ref, x_ref, wq_hbm, wk_hbm, wv_hbm, wo_hbm, wup_hbm, wdown_hbm,
    out_ref,
    wq, wk, wv, wo, wup, wdown, wvt, nrm, own, rbuf, xbuf, qt, ks, vt, acc, top, chunk_top, st, ps, mix, w_sem,
    s_sem, r_sem, xs_sem, xr_sem, bs_sem, br_sem,
):
    weights = [(wq_hbm, wq), (wk_hbm, wk), (wv_hbm, wv), (wo_hbm, wo), (wup_hbm, wup), (wdown_hbm, wdown)]

    def fetch(k):
        return pltpu.make_async_copy(weights[k][0], weights[k][1], w_sem.at[k])

    for k in range(3):
        fetch(k).start()

    g, d = lax.axis_index("group"), lax.axis_index("dom")
    y, z = d // 4, d % 4
    up_y, dn_y = (y + 1) % 4 * 4 + z, (y + 3) % 4 * 4 + z
    up_z, dn_z = y * 4 + (z + 1) % 4, y * 4 + (z + 3) % 4
    towards = [(g, up_y), (g, up_z), (g, dn_y), (g, dn_z)]
    up_x, dn_x, sibling = ((g + 2) % 8, d), ((g + 6) % 8, d), (g + 1 - 2 * (g % 2), d)

    barrier = pltpu.get_barrier_semaphore()
    for other in [*towards, up_x, dn_x, sibling]:
        pl.semaphore_signal(barrier, inc=1, device_id=other, device_id_type=MESH)

    normed = rms(x_ref[...].astype(F32))
    nrm[...] = normed
    row = lax.broadcasted_iota(jnp.int32, (BLK, D), 0)
    lane = lax.broadcasted_iota(jnp.int32, (BLK, D), 1)
    flag = jnp.where((lane == 0) | (lane == 64), FLAG, 0.0)
    for b in range(4):
        part = normed[b * BLK:(b + 1) * BLK].astype(F32)
        flagged = jnp.where(row < len_ref[b], part, flag).astype(BF16)
        rbuf[b * BLK:(b + 1) * BLK, :] = flagged
        own[b] = flagged

    pl.semaphore_wait(barrier, 7)

    def send(n, link):
        arrival, other = SOURCE[n]
        return pltpu.make_async_remote_copy(
            src_ref=rbuf.at[pl.ds((arrival + 1) * TOK + (link ^ other) * BLK, BLK)],
            dst_ref=rbuf.at[pl.ds((n + 1) * TOK + link * BLK, BLK)],
            send_sem=s_sem.at[n, link], recv_sem=r_sem.at[n, link],
            device_id=towards[link], device_id_type=MESH,
        )

    def start_after(arrival):
        for n in range(ROUNDS - 1):
            if SOURCE[n][0] == arrival:
                for link in range(4):
                    send(n, link).start()

    def step(arrival):
        for link in range(4):
            send(arrival, link).wait_recv()
        start_after(arrival)

    def send_x(s, way):
        return pltpu.make_async_remote_copy(
            src_ref=own.at[pl.ds(2 * way, 2)] if s == 0 else xbuf.at[pl.ds(4 * s + 2 * way, 2)],
            dst_ref=xbuf.at[pl.ds(4 * s + 4 + 2 * way, 2)],
            send_sem=xs_sem.at[s, way], recv_sem=xr_sem.at[s, way],
            device_id=(up_x, dn_x)[way], device_id_type=MESH,
        )

    def send_sibling(s):
        return pltpu.make_async_remote_copy(
            src_ref=own if s == 0 else xbuf.at[pl.ds(4 * s, 4)],
            dst_ref=xbuf.at[pl.ds(16 + 4 * s, 4)],
            send_sem=bs_sem.at[s], recv_sem=br_sem.at[s],
            device_id=sibling, device_id_type=MESH,
        )

    def step_x(s):
        for way in range(2):
            send_x(s - 1, way).wait_recv()
            if s < 3:
                send_x(s, way).start()
        send_sibling(s).start()

    start_after(-1)
    for way in range(2):
        send_x(0, way).start()
    send_sibling(0).start()
    for k in range(3, 6):
        fetch(k).start()

    fetch(0).wait()
    q_all = dot_t(jnp.transpose(wq[...].astype(F32)).astype(BF16), nrm[...]) * (math.log2(math.e) / 8.0)
    q_all = q_all.astype(BF16)
    ones = jnp.ones((HEAD, TOK), BF16)
    for h in range(HEADS):
        at = (h % 2) * HEAD
        qt[h, at:at + HEAD, :] = q_all[h * HEAD:(h + 1) * HEAD]
        qt[h, HEAD - at:HEAD - at + HEAD, :] = ones
        vt[h, HEAD:VROWS, :] = jnp.ones((VROWS - HEAD, 2 * TOK), BF16)
    fetch(1).wait()
    fetch(2).wait()
    wvt[...] = jnp.transpose(wv[...].astype(F32)).astype(BF16)
    acc[...] = jnp.zeros_like(acc)
    top[...] = jnp.full_like(top, NEG)

    def keys_of(rows, unused=None):
        n = rows.shape[0]
        ks[0:n, :] = dot(rows, wk[...]).astype(BF16)
        values = dot_t(wvt[...], rows).astype(BF16)
        for h in range(HEADS):
            vt[h, 0:HEAD, 0:n] = values[h * HEAD:(h + 1) * HEAD]
        mask = jnp.where(rows[:, 0:BLK].astype(F32) > FLAG / 2, NEG, 0.0)
        if unused is not None:
            mask = jnp.where(unused, NEG, mask)
        return mask.astype(BF16)

    def scores(h, at, n, mask, q):
        lane = lax.broadcasted_iota(jnp.int32, (n, BLK), 1)
        pair = ks[at:at + n, (h // 2) * BLK:(h // 2 + 1) * BLK]
        mine = (lane < HEAD) if h % 2 == 0 else (lane >= HEAD)
        return dot(jnp.where(mine, pair, mask[at:at + n]), q)

    def pipeline(units, first, second, third):
        first(0)
        first(1)
        second(0)
        for u in range(units):
            if u + 1 < units:
                second(u + 1)
            if u + 2 < units:
                first(u + 2)
            third(u)

    def attend(rows):
        n = rows.shape[0]
        mask = keys_of(rows)

        def first(h):
            s = scores(h, 0, n, mask, qt[h])
            st[h % 2, 0:n] = s
            chunk_top[h % 2] = jnp.max(s.reshape(n // 8, 8, TOK), axis=0)

        def second(h):
            old = top[h]
            new = jnp.maximum(old, jnp.max(chunk_top[h % 2], axis=0, keepdims=True))
            top[h] = new
            ps[h % 2, 0:n] = jnp.exp2(st[h % 2, 0:n] - new).astype(BF16)
            acc[h] = acc[h] * jnp.exp2(old - new)

        def third(h):
            acc[h] += dot(vt[h, :, 0:n], ps[h % 2, 0:n])

        pipeline(HEADS, first, second, third)

    def cross():
        picked, unused = [], []
        for b in range(4):
            for c in range(2):
                block = blocks_ref[c, b]
                group, local = lax.div(block, 64), lax.rem(block, 4)
                apart = (lax.div(g, 2) - lax.div(group, 2)) * (1 - 2 * lax.div(local, 2))
                slot = lax.rem(group + g, 2) * 16 + lax.rem(apart + 4, 4) * 4 + local
                picked.append(xbuf[slot])
            at = lax.broadcasted_iota(jnp.int32, (2 * BLK, BLK), 0) // BLK
            unused.append(at >= count_ref[b])
        mask = keys_of(jnp.concatenate(picked, axis=0), jnp.concatenate(unused, axis=0))
        n = 2 * BLK

        def first(u):
            h, b = u % HEADS, u // HEADS
            st[u % 2, 0:n, 0:BLK] = scores(h, b * n, n, mask, qt[h, :, b * BLK:(b + 1) * BLK])

        def second(u):
            s = st[u % 2, 0:n, 0:BLK]
            ps[u % 2, 0:n, 0:BLK] = jnp.exp2(s - jnp.max(s, axis=0, keepdims=True)).astype(BF16)

        def third(u):
            h, b = u % HEADS, u // HEADS
            o = dot(vt[h, :, b * n:(b + 1) * n], ps[u % 2, 0:n, 0:BLK])
            mix[h * HEAD:(h + 1) * HEAD, b * BLK:(b + 1) * BLK] = o[0:HEAD] / o[HEAD:HEAD + 1]

        pipeline(4 * HEADS, first, second, third)

    attend(rbuf[0:TOK, :])

    def round_(r, carry):
        for k in range(1, 8):
            @pl.when(r == k)
            def _(k=k):
                step(2 * k - 2)
                step(2 * k - 1)
                if 2 <= k < 5:
                    step_x(k - 1)
        attend(rbuf[pl.ds(pl.multiple_of((2 * r - 1) * TOK, TOK), 2 * TOK), :])
        return carry

    lax.fori_loop(1, 8, round_, 0)

    for s in range(4):
        send_sibling(s).wait_recv()
    cross()
    step(ROUNDS - 2)
    attend(rbuf[(ROUNDS - 1) * TOK:ROUNDS * TOK, :])

    for n in range(ROUNDS - 1):
        for link in range(4):
            send(n, link).wait_send()
    for s in range(3):
        for way in range(2):
            send_x(s, way).wait_send()
    for s in range(4):
        send_sibling(s).wait_send()

    for h in range(HEADS):
        at = slice(h * HEAD, (h + 1) * HEAD)
        mix[at, :] = mix[at, :] + acc[h, 0:HEAD] / acc[h, HEAD:HEAD + 1]
    mixed = jnp.transpose(mix[...]).astype(BF16)
    for k in range(3, 6):
        fetch(k).wait()
    resid = (x_ref[...].astype(F32) + dot(mixed, wo[...])).astype(BF16)
    normed_two = rms(resid.astype(F32))
    total = resid.astype(F32)
    for k in range(FF // TOK):
        cols = slice(k * TOK, (k + 1) * TOK)
        hidden = jax.nn.gelu(dot(normed_two, wup[:, cols])).astype(BF16)
        total = total + dot(hidden, wdown[cols, :])
    out_ref[...] = total.astype(BF16)


def body(features, w_query, w_key, w_value, w_out, w_up, w_down, block_len, cross_blocks, cross_count):
    smem = pl.BlockSpec(memory_space=pltpu.SMEM)
    vmem = pl.BlockSpec(memory_space=pltpu.VMEM)
    hbm = pl.BlockSpec(memory_space=pl.ANY)
    dma = pltpu.SemaphoreType.DMA
    return pl.pallas_call(
        kernel,
        out_shape=jax.ShapeDtypeStruct((TOK, D), BF16),
        in_specs=[smem] * 3 + [vmem] + [hbm] * 6,
        out_specs=vmem,
        scratch_shapes=[
            pltpu.VMEM((D, D), BF16), pltpu.VMEM((D, D), BF16), pltpu.VMEM((D, D), BF16), pltpu.VMEM((D, D), BF16),
            pltpu.VMEM((D, FF), BF16), pltpu.VMEM((FF, D), BF16),
            pltpu.VMEM((D, D), BF16),
            pltpu.VMEM((TOK, D), BF16),
            pltpu.VMEM((4, BLK, D), BF16),
            pltpu.VMEM((ROUNDS * TOK, D), BF16),
            pltpu.VMEM((32, BLK, D), BF16),
            pltpu.VMEM((HEADS, 2 * HEAD, TOK), BF16),
            pltpu.VMEM((2 * TOK, D), BF16),
            pltpu.VMEM((HEADS, VROWS, 2 * TOK), BF16),
            pltpu.VMEM((HEADS, VROWS, TOK), F32),
            pltpu.VMEM((HEADS, 1, TOK), F32),
            pltpu.VMEM((2, 8, TOK), F32),
            pltpu.VMEM((2, 2 * TOK, TOK), F32),
            pltpu.VMEM((2, 2 * TOK, TOK), BF16),
            pltpu.VMEM((D, TOK), F32),
            dma((6,)),
            dma((ROUNDS - 1, 4)), dma((ROUNDS - 1, 4)),
            dma((3, 2)), dma((3, 2)), dma((4,)), dma((4,)),
        ],
        compiler_params=pltpu.CompilerParams(
            collective_id=0, has_side_effects=True, vmem_limit_bytes=60 * 2**20
        ),
        name="layer",
    )(block_len, cross_blocks.T, cross_count, features, w_query, w_key, w_value, w_out, w_up, w_down)


def solution(mesh):
    both = P(("group", "dom"))
    rows = P(("group", "dom"), None)
    return jax.shard_map(
        body,
        mesh=mesh,
        in_specs=(rows, P(), P(), P(), P(), P(), P(), both, rows, both),
        out_specs=rows,
        check_vma=False,
    )
```

```python
import functools
import math

import jax
import jax.numpy as jnp
from jax import lax
from jax.experimental import pallas as pl
from jax.experimental.pallas import tpu as pltpu
from jax.sharding import PartitionSpec as P

F32, BF16 = jnp.float32, jnp.bfloat16
MESH = pl.DeviceIdType.MESH
HEADS = 8
HEAD = 64
BLK = 128
TOK = 512
D = 512
FF = 2048
VROWS = 80
ROUNDS = 16
NEG = -1e30
FLAG = 64.0
SOURCE = (
    (-1, 0), (-1, 2), (-1, 1), (-1, 3), (0, 0), (0, 1), (0, 3), (1, 3),
    (1, 1), (2, 0), (4, 1), (4, 3), (5, 0), (7, 0), (10, 0),
)


def dot(a, b):
    return jnp.dot(a, b, preferred_element_type=F32)


def dot_t(a, b):
    return lax.dot_general(a, b, (((1,), (1,)), ((), ())), preferred_element_type=F32)


def rms(wide):
    return (wide * lax.rsqrt(jnp.mean(wide * wide, axis=-1, keepdims=True) + 1e-06)).astype(BF16)


def kernel(
    len_ref, blocks_ref, count_ref, x_ref, wq_hbm, wk_hbm, wv_hbm, wo_hbm, wup_hbm, wdown_hbm,
    out_ref,
    wq, wk, wv, wo, wup, wdown, wvt, nrm, own, rbuf, xbuf, qt, ks, vt, acc, top, chunk_top, st, ps, mix, w_sem,
    s_sem, r_sem, xs_sem, xr_sem, bs_sem, br_sem,
):
    weights = [(wq_hbm, wq), (wk_hbm, wk), (wv_hbm, wv), (wo_hbm, wo), (wup_hbm, wup), (wdown_hbm, wdown)]

    def fetch(k):
        return pltpu.make_async_copy(weights[k][0], weights[k][1], w_sem.at[k])

    for k in range(3):
        fetch(k).start()

    g, d = lax.axis_index("group"), lax.axis_index("dom")
    y, z = d // 4, d % 4
    up_y, dn_y = (y + 1) % 4 * 4 + z, (y + 3) % 4 * 4 + z
    up_z, dn_z = y * 4 + (z + 1) % 4, y * 4 + (z + 3) % 4
    towards = [(g, up_y), (g, up_z), (g, dn_y), (g, dn_z)]
    up_x, dn_x, sibling = ((g + 2) % 8, d), ((g + 6) % 8, d), (g + 1 - 2 * (g % 2), d)

    barrier = pltpu.get_barrier_semaphore()
    for other in [*towards, up_x, dn_x, sibling]:
        pl.semaphore_signal(barrier, inc=1, device_id=other, device_id_type=MESH)

    normed = rms(x_ref[...].astype(F32))
    nrm[...] = normed
    row = lax.broadcasted_iota(jnp.int32, (BLK, D), 0)
    lane = lax.broadcasted_iota(jnp.int32, (BLK, D), 1)
    flag = jnp.where((lane == 0) | (lane == 64), FLAG, 0.0)
    for b in range(4):
        part = normed[b * BLK:(b + 1) * BLK].astype(F32)
        flagged = jnp.where(row < len_ref[b], part, flag).astype(BF16)
        rbuf[b * BLK:(b + 1) * BLK, :] = flagged
        own[b] = flagged

    pl.semaphore_wait(barrier, 7)

    def send(n, link):
        arrival, other = SOURCE[n]
        return pltpu.make_async_remote_copy(
            src_ref=rbuf.at[pl.ds((arrival + 1) * TOK + (link ^ other) * BLK, BLK)],
            dst_ref=rbuf.at[pl.ds((n + 1) * TOK + link * BLK, BLK)],
            send_sem=s_sem.at[n, link], recv_sem=r_sem.at[n, link],
            device_id=towards[link], device_id_type=MESH,
        )

    def start(n):
        if n < ROUNDS - 1:
            for link in range(4):
                send(n, link).start()

    def arrive(n):
        for link in range(4):
            send(n, link).wait_recv()

    def send_x(s, way):
        return pltpu.make_async_remote_copy(
            src_ref=own.at[pl.ds(2 * way, 2)] if s == 0 else xbuf.at[pl.ds(4 * s + 2 * way, 2)],
            dst_ref=xbuf.at[pl.ds(4 * s + 4 + 2 * way, 2)],
            send_sem=xs_sem.at[s, way], recv_sem=xr_sem.at[s, way],
            device_id=(up_x, dn_x)[way], device_id_type=MESH,
        )

    def send_sibling(s):
        return pltpu.make_async_remote_copy(
            src_ref=own if s == 0 else xbuf.at[pl.ds(4 * s, 4)],
            dst_ref=xbuf.at[pl.ds(16 + 4 * s, 4)],
            send_sem=bs_sem.at[s], recv_sem=br_sem.at[s],
            device_id=sibling, device_id_type=MESH,
        )

    def step_x(s):
        for way in range(2):
            send_x(s - 1, way).wait_recv()
            if s < 3:
                send_x(s, way).start()
        send_sibling(s).start()

    start(0)
    for way in range(2):
        send_x(0, way).start()
    send_sibling(0).start()
    for k in range(3, 6):
        fetch(k).start()

    fetch(0).wait()
    q_all = dot_t(jnp.transpose(wq[...].astype(F32)).astype(BF16), nrm[...]) * (math.log2(math.e) / 8.0)
    q_all = q_all.astype(BF16)
    ones = jnp.ones((HEAD, TOK), BF16)
    for h in range(HEADS):
        at = (h % 2) * HEAD
        qt[h, at:at + HEAD, :] = q_all[h * HEAD:(h + 1) * HEAD]
        qt[h, HEAD - at:HEAD - at + HEAD, :] = ones
        vt[h, HEAD:VROWS, :] = jnp.ones((VROWS - HEAD, 2 * TOK), BF16)
    fetch(1).wait()
    fetch(2).wait()
    wvt[...] = jnp.transpose(wv[...].astype(F32)).astype(BF16)
    acc[...] = jnp.zeros_like(acc)
    top[...] = jnp.full_like(top, NEG)

    def keys_of(rows, unused=None):
        n = rows.shape[0]
        ks[0:n, :] = dot(rows, wk[...]).astype(BF16)
        values = dot_t(wvt[...], rows).astype(BF16)
        for h in range(HEADS):
            vt[h, 0:HEAD, 0:n] = values[h * HEAD:(h + 1) * HEAD]
        mask = jnp.where(rows[:, 0:BLK].astype(F32) > FLAG / 2, NEG, 0.0)
        if unused is not None:
            mask = jnp.where(unused, NEG, mask)
        return mask.astype(BF16)

    def scores(h, at, n, mask, q):
        lane = lax.broadcasted_iota(jnp.int32, (n, BLK), 1)
        pair = ks[at:at + n, (h // 2) * BLK:(h // 2 + 1) * BLK]
        mine = (lane < HEAD) if h % 2 == 0 else (lane >= HEAD)
        return dot(jnp.where(mine, pair, mask[at:at + n]), q)

    def pipeline(units, first, second, third):
        first(0)
        first(1)
        second(0)
        for u in range(units):
            if u + 1 < units:
                second(u + 1)
            if u + 2 < units:
                first(u + 2)
            third(u)

    def attend(rows):
        n = rows.shape[0]
        mask = keys_of(rows)

        def first(h):
            s = scores(h, 0, n, mask, qt[h])
            st[h % 2, 0:n] = s
            chunk_top[h % 2] = jnp.max(s.reshape(n // 8, 8, TOK), axis=0)

        def second(h):
            old = top[h]
            new = jnp.maximum(old, jnp.max(chunk_top[h % 2], axis=0, keepdims=True))
            top[h] = new
            ps[h % 2, 0:n] = jnp.exp2(st[h % 2, 0:n] - new).astype(BF16)
            acc[h] = acc[h] * jnp.exp2(old - new)

        def third(h):
            acc[h] += dot(vt[h, :, 0:n], ps[h % 2, 0:n])

        pipeline(HEADS, first, second, third)

    def cross():
        picked, unused = [], []
        for b in range(4):
            for c in range(2):
                block = blocks_ref[c, b]
                group, local = lax.div(block, 64), lax.rem(block, 4)
                apart = (lax.div(g, 2) - lax.div(group, 2)) * (1 - 2 * lax.div(local, 2))
                slot = lax.rem(group + g, 2) * 16 + lax.rem(apart + 4, 4) * 4 + local
                picked.append(xbuf[slot])
            at = lax.broadcasted_iota(jnp.int32, (2 * BLK, BLK), 0) // BLK
            unused.append(at >= count_ref[b])
        mask = keys_of(jnp.concatenate(picked, axis=0), jnp.concatenate(unused, axis=0))
        n = 2 * BLK

        def first(u):
            h, b = u % HEADS, u // HEADS
            st[u % 2, 0:n, 0:BLK] = scores(h, b * n, n, mask, qt[h, :, b * BLK:(b + 1) * BLK])

        def second(u):
            s = st[u % 2, 0:n, 0:BLK]
            ps[u % 2, 0:n, 0:BLK] = jnp.exp2(s - jnp.max(s, axis=0, keepdims=True)).astype(BF16)

        def third(u):
            h, b = u % HEADS, u // HEADS
            o = dot(vt[h, :, b * n:(b + 1) * n], ps[u % 2, 0:n, 0:BLK])
            mix[h * HEAD:(h + 1) * HEAD, b * BLK:(b + 1) * BLK] = o[0:HEAD] / o[HEAD:HEAD + 1]

        pipeline(4 * HEADS, first, second, third)

    start(1)

    def single(r, carry):
        @pl.when(r == 1)
        def _():
            start(2)
            arrive(0)
            start(3)
            start(4)

        @pl.when(r == 2)
        def _():
            arrive(1)
            start(5)
            start(6)

        attend(rbuf[pl.ds(pl.multiple_of(r * TOK, TOK), TOK), :])
        return carry

    lax.fori_loop(0, 3, single, 0)

    def double(r, carry):
        for k in range(6):
            @pl.when(r == k)
            def _(k=k):
                arrive(2 * k + 2)
                if k < 3:
                    start(2 * k + 7)
                arrive(2 * k + 3)
                if k < 3:
                    start(2 * k + 8)
                else:
                    start(k + 10)
                if k in (0, 2, 4):
                    step_x(k // 2 + 1)
        attend(rbuf[pl.ds(pl.multiple_of((2 * r + 3) * TOK, TOK), 2 * TOK), :])
        return carry

    lax.fori_loop(0, 6, double, 0)

    for s in range(4):
        send_sibling(s).wait_recv()
    cross()
    arrive(ROUNDS - 2)
    attend(rbuf[(ROUNDS - 1) * TOK:ROUNDS * TOK, :])

    for n in range(ROUNDS - 1):
        for link in range(4):
            send(n, link).wait_send()
    for s in range(3):
        for way in range(2):
            send_x(s, way).wait_send()
    for s in range(4):
        send_sibling(s).wait_send()

    for h in range(HEADS):
        at = slice(h * HEAD, (h + 1) * HEAD)
        mix[at, :] = mix[at, :] + acc[h, 0:HEAD] / acc[h, HEAD:HEAD + 1]
    mixed = jnp.transpose(mix[...]).astype(BF16)
    for k in range(3, 6):
        fetch(k).wait()
    resid = (x_ref[...].astype(F32) + dot(mixed, wo[...])).astype(BF16)
    normed_two = rms(resid.astype(F32))
    total = resid.astype(F32)
    for k in range(FF // TOK):
        cols = slice(k * TOK, (k + 1) * TOK)
        hidden = jax.nn.gelu(dot(normed_two, wup[:, cols])).astype(BF16)
        total = total + dot(hidden, wdown[cols, :])
    out_ref[...] = total.astype(BF16)


def body(features, w_query, w_key, w_value, w_out, w_up, w_down, block_len, cross_blocks, cross_count):
    smem = pl.BlockSpec(memory_space=pltpu.SMEM)
    vmem = pl.BlockSpec(memory_space=pltpu.VMEM)
    hbm = pl.BlockSpec(memory_space=pl.ANY)
    dma = pltpu.SemaphoreType.DMA
    return pl.pallas_call(
        kernel,
        out_shape=jax.ShapeDtypeStruct((TOK, D), BF16),
        in_specs=[smem] * 3 + [vmem] + [hbm] * 6,
        out_specs=vmem,
        scratch_shapes=[
            pltpu.VMEM((D, D), BF16), pltpu.VMEM((D, D), BF16), pltpu.VMEM((D, D), BF16), pltpu.VMEM((D, D), BF16),
            pltpu.VMEM((D, FF), BF16), pltpu.VMEM((FF, D), BF16),
            pltpu.VMEM((D, D), BF16),
            pltpu.VMEM((TOK, D), BF16),
            pltpu.VMEM((4, BLK, D), BF16),
            pltpu.VMEM((ROUNDS * TOK, D), BF16),
            pltpu.VMEM((32, BLK, D), BF16),
            pltpu.VMEM((HEADS, 2 * HEAD, TOK), BF16),
            pltpu.VMEM((2 * TOK, D), BF16),
            pltpu.VMEM((HEADS, VROWS, 2 * TOK), BF16),
            pltpu.VMEM((HEADS, VROWS, TOK), F32),
            pltpu.VMEM((HEADS, 1, TOK), F32),
            pltpu.VMEM((2, 8, TOK), F32),
            pltpu.VMEM((2, 2 * TOK, TOK), F32),
            pltpu.VMEM((2, 2 * TOK, TOK), BF16),
            pltpu.VMEM((D, TOK), F32),
            dma((6,)),
            dma((ROUNDS - 1, 4)), dma((ROUNDS - 1, 4)),
            dma((3, 2)), dma((3, 2)), dma((4,)), dma((4,)),
        ],
        compiler_params=pltpu.CompilerParams(
            collective_id=0, has_side_effects=True, vmem_limit_bytes=60 * 2**20
        ),
        name="layer",
    )(block_len, cross_blocks.T, cross_count, features, w_query, w_key, w_value, w_out, w_up, w_down)


def solution(mesh):
    both = P(("group", "dom"))
    rows = P(("group", "dom"), None)
    return jax.shard_map(
        body,
        mesh=mesh,
        in_specs=(rows, P(), P(), P(), P(), P(), P(), both, rows, both),
        out_specs=rows,
        check_vma=False,
    )
```

```python
import functools
import math

import jax
import jax.numpy as jnp
from jax import lax
from jax.experimental import pallas as pl
from jax.experimental.pallas import tpu as pltpu
from jax.sharding import PartitionSpec as P

F32, BF16 = jnp.float32, jnp.bfloat16
MESH = pl.DeviceIdType.MESH
HEADS = 8
HEAD = 64
BLK = 128
TOK = 512
D = 512
FF = 2048
VROWS = 80
ROUNDS = 16
NEG = -1e30
FLAG = 64.0
SOURCE = (
    (-1, 0), (-1, 2), (-1, 1), (-1, 3), (0, 0), (0, 1), (0, 3), (1, 3),
    (1, 1), (2, 0), (4, 1), (4, 3), (5, 0), (7, 0), (10, 0),
)


def dot(a, b):
    return jnp.dot(a, b, preferred_element_type=F32)


def dot_t(a, b):
    return lax.dot_general(a, b, (((1,), (1,)), ((), ())), preferred_element_type=F32)


def rms(wide):
    return (wide * lax.rsqrt(jnp.mean(wide * wide, axis=-1, keepdims=True) + 1e-06)).astype(BF16)


def kernel(
    len_ref, blocks_ref, count_ref, x_ref, wq_hbm, wk_hbm, wv_hbm, wo_hbm, wup_hbm, wdown_hbm,
    out_ref,
    wq, wk, wv, wo, wup, wdown, wvt, nrm, own, rbuf, xbuf, qt, ks, vt, acc, top, chunk_top, st, ps, mix, w_sem,
    s_sem, r_sem, xs_sem, xr_sem, bs_sem, br_sem,
):
    weights = [(wq_hbm, wq), (wk_hbm, wk), (wv_hbm, wv), (wo_hbm, wo), (wup_hbm, wup), (wdown_hbm, wdown)]

    def fetch(k):
        return pltpu.make_async_copy(weights[k][0], weights[k][1], w_sem.at[k])

    for k in range(3):
        fetch(k).start()

    g, d = lax.axis_index("group"), lax.axis_index("dom")
    y, z = d // 4, d % 4
    up_y, dn_y = (y + 1) % 4 * 4 + z, (y + 3) % 4 * 4 + z
    up_z, dn_z = y * 4 + (z + 1) % 4, y * 4 + (z + 3) % 4
    towards = [(g, up_y), (g, up_z), (g, dn_y), (g, dn_z)]
    up_x, dn_x, sibling = ((g + 2) % 8, d), ((g + 6) % 8, d), (g + 1 - 2 * (g % 2), d)

    barrier = pltpu.get_barrier_semaphore()
    for other in [*towards, up_x, dn_x, sibling]:
        pl.semaphore_signal(barrier, inc=1, device_id=other, device_id_type=MESH)

    normed = rms(x_ref[...].astype(F32))
    nrm[...] = normed
    row = lax.broadcasted_iota(jnp.int32, (BLK, D), 0)
    lane = lax.broadcasted_iota(jnp.int32, (BLK, D), 1)
    flag = jnp.where((lane == 0) | (lane == 64), FLAG, 0.0)
    for b in range(4):
        part = normed[b * BLK:(b + 1) * BLK].astype(F32)
        flagged = jnp.where(row < len_ref[b], part, flag).astype(BF16)
        rbuf[b * BLK:(b + 1) * BLK, :] = flagged
        own[b] = flagged

    pl.semaphore_wait(barrier, 7)

    def whole(ref, sem):
        return pltpu.make_async_remote_copy(
            src_ref=ref, dst_ref=ref, send_sem=sem, recv_sem=sem, device_id=sibling, device_id_type=MESH
        )

    def landed(ref, sem):
        whole(ref, sem).wait_recv()

    def left(ref, sem):
        whole(ref, sem).wait_send()

    def send(n, link):
        arrival, other = SOURCE[n]
        return pltpu.make_async_remote_copy(
            src_ref=rbuf.at[pl.ds((arrival + 1) * TOK + (link ^ other) * BLK, BLK)],
            dst_ref=rbuf.at[pl.ds((n + 1) * TOK + link * BLK, BLK)],
            send_sem=s_sem, recv_sem=r_sem.at[n],
            device_id=towards[link], device_id_type=MESH,
        )

    def start(n):
        if n < ROUNDS - 1:
            for link in range(4):
                send(n, link).start()

    def arrive(n):
        landed(rbuf.at[pl.ds((n + 1) * TOK, TOK)], r_sem.at[n])

    def send_x(s, way):
        return pltpu.make_async_remote_copy(
            src_ref=own.at[pl.ds(2 * way, 2)] if s == 0 else xbuf.at[pl.ds(4 * s + 2 * way, 2)],
            dst_ref=xbuf.at[pl.ds(4 * s + 4 + 2 * way, 2)],
            send_sem=xs_sem, recv_sem=xr_sem.at[s],
            device_id=(up_x, dn_x)[way], device_id_type=MESH,
        )

    def send_sibling(s):
        return pltpu.make_async_remote_copy(
            src_ref=own if s == 0 else xbuf.at[pl.ds(4 * s, 4)],
            dst_ref=xbuf.at[pl.ds(16 + 4 * s, 4)],
            send_sem=bs_sem, recv_sem=br_sem,
            device_id=sibling, device_id_type=MESH,
        )

    def step_x(s):
        landed(xbuf.at[pl.ds(4 * s, 4)], xr_sem.at[s - 1])
        if s < 3:
            for way in range(2):
                send_x(s, way).start()
        send_sibling(s).start()

    start(0)
    for way in range(2):
        send_x(0, way).start()
    send_sibling(0).start()
    for k in range(3, 6):
        fetch(k).start()

    fetch(0).wait()
    q_all = dot_t(jnp.transpose(wq[...].astype(F32)).astype(BF16), nrm[...]) * (math.log2(math.e) / 8.0)
    q_all = q_all.astype(BF16)
    ones = jnp.ones((HEAD, TOK), BF16)
    for h in range(HEADS):
        at = (h % 2) * HEAD
        qt[h, at:at + HEAD, :] = q_all[h * HEAD:(h + 1) * HEAD]
        qt[h, HEAD - at:HEAD - at + HEAD, :] = ones
        vt[h, HEAD:VROWS, :] = jnp.ones((VROWS - HEAD, 2 * TOK), BF16)
    fetch(1).wait()
    fetch(2).wait()
    wvt[...] = jnp.transpose(wv[...].astype(F32)).astype(BF16)
    acc[...] = jnp.zeros_like(acc)
    top[...] = jnp.full_like(top, NEG)

    def keys_of(rows, unused=None):
        n = rows.shape[0]
        ks[0:n, :] = dot(rows, wk[...]).astype(BF16)
        values = dot_t(wvt[...], rows).astype(BF16)
        for h in range(HEADS):
            vt[h, 0:HEAD, 0:n] = values[h * HEAD:(h + 1) * HEAD]
        mask = jnp.where(rows[:, 0:BLK].astype(F32) > FLAG / 2, NEG, 0.0)
        if unused is not None:
            mask = jnp.where(unused, NEG, mask)
        return mask.astype(BF16)

    def scores(h, at, n, mask, q):
        lane = lax.broadcasted_iota(jnp.int32, (n, BLK), 1)
        pair = ks[at:at + n, (h // 2) * BLK:(h // 2 + 1) * BLK]
        mine = (lane < HEAD) if h % 2 == 0 else (lane >= HEAD)
        return dot(jnp.where(mine, pair, mask[at:at + n]), q)

    def pipeline(units, first, second, third):
        first(0)
        first(1)
        second(0)
        for u in range(units):
            if u + 1 < units:
                second(u + 1)
            if u + 2 < units:
                first(u + 2)
            third(u)

    def attend(rows):
        n = rows.shape[0]
        mask = keys_of(rows)

        def first(h):
            s = scores(h, 0, n, mask, qt[h])
            st[h % 2, 0:n] = s
            chunk_top[h % 2] = jnp.max(s.reshape(n // 8, 8, TOK), axis=0)

        def second(h):
            old = top[h]
            new = jnp.maximum(old, jnp.max(chunk_top[h % 2], axis=0, keepdims=True))
            top[h] = new
            ps[h % 2, 0:n] = jnp.exp2(st[h % 2, 0:n] - new).astype(BF16)
            acc[h] = acc[h] * jnp.exp2(old - new)

        def third(h):
            acc[h] += dot(vt[h, :, 0:n], ps[h % 2, 0:n])

        pipeline(HEADS, first, second, third)

    def cross():
        picked, unused = [], []
        for b in range(4):
            for c in range(2):
                block = blocks_ref[c, b]
                group, local = lax.div(block, 64), lax.rem(block, 4)
                apart = (lax.div(g, 2) - lax.div(group, 2)) * (1 - 2 * lax.div(local, 2))
                slot = lax.rem(group + g, 2) * 16 + lax.rem(apart + 4, 4) * 4 + local
                picked.append(xbuf[slot])
            at = lax.broadcasted_iota(jnp.int32, (2 * BLK, BLK), 0) // BLK
            unused.append(at >= count_ref[b])
        mask = keys_of(jnp.concatenate(picked, axis=0), jnp.concatenate(unused, axis=0))
        n = 2 * BLK

        def first(u):
            h, b = u % HEADS, u // HEADS
            st[u % 2, 0:n, 0:BLK] = scores(h, b * n, n, mask, qt[h, :, b * BLK:(b + 1) * BLK])

        def second(u):
            s = st[u % 2, 0:n, 0:BLK]
            ps[u % 2, 0:n, 0:BLK] = jnp.exp2(s - jnp.max(s, axis=0, keepdims=True)).astype(BF16)

        def third(u):
            h, b = u % HEADS, u // HEADS
            o = dot(vt[h, :, b * n:(b + 1) * n], ps[u % 2, 0:n, 0:BLK])
            mix[h * HEAD:(h + 1) * HEAD, b * BLK:(b + 1) * BLK] = o[0:HEAD] / o[HEAD:HEAD + 1]

        pipeline(4 * HEADS, first, second, third)

    start(1)

    def single(r, carry):
        @pl.when(r == 1)
        def _():
            start(2)
            arrive(0)
            start(3)
            start(4)

        @pl.when(r == 2)
        def _():
            arrive(1)
            start(5)
            start(6)

        attend(rbuf[pl.ds(pl.multiple_of(r * TOK, TOK), TOK), :])
        return carry

    lax.fori_loop(0, 3, single, 0)

    def double(r, carry):
        for k in range(6):
            @pl.when(r == k)
            def _(k=k):
                arrive(2 * k + 2)
                if k < 3:
                    start(2 * k + 7)
                arrive(2 * k + 3)
                if k < 3:
                    start(2 * k + 8)
                else:
                    start(k + 10)
                if k in (0, 2, 4):
                    step_x(k // 2 + 1)
        attend(rbuf[pl.ds(pl.multiple_of((2 * r + 3) * TOK, TOK), 2 * TOK), :])
        return carry

    lax.fori_loop(0, 6, double, 0)

    landed(xbuf.at[pl.ds(16, 16)], br_sem)
    cross()
    arrive(ROUNDS - 2)
    attend(rbuf[(ROUNDS - 1) * TOK:ROUNDS * TOK, :])

    left(rbuf.at[pl.ds(0, (ROUNDS - 1) * TOK)], s_sem)
    left(xbuf.at[pl.ds(0, 12)], xs_sem)
    left(xbuf.at[pl.ds(0, 16)], bs_sem)

    for h in range(HEADS):
        at = slice(h * HEAD, (h + 1) * HEAD)
        mix[at, :] = mix[at, :] + acc[h, 0:HEAD] / acc[h, HEAD:HEAD + 1]
    mixed = jnp.transpose(mix[...]).astype(BF16)
    for k in range(3, 6):
        fetch(k).wait()
    resid = (x_ref[...].astype(F32) + dot(mixed, wo[...])).astype(BF16)
    normed_two = rms(resid.astype(F32))
    total = resid.astype(F32)
    for k in range(FF // TOK):
        cols = slice(k * TOK, (k + 1) * TOK)
        hidden = jax.nn.gelu(dot(normed_two, wup[:, cols])).astype(BF16)
        total = total + dot(hidden, wdown[cols, :])
    out_ref[...] = total.astype(BF16)


def body(features, w_query, w_key, w_value, w_out, w_up, w_down, block_len, cross_blocks, cross_count):
    smem = pl.BlockSpec(memory_space=pltpu.SMEM)
    vmem = pl.BlockSpec(memory_space=pltpu.VMEM)
    hbm = pl.BlockSpec(memory_space=pl.ANY)
    dma = pltpu.SemaphoreType.DMA
    return pl.pallas_call(
        kernel,
        out_shape=jax.ShapeDtypeStruct((TOK, D), BF16),
        in_specs=[smem] * 3 + [vmem] + [hbm] * 6,
        out_specs=vmem,
        scratch_shapes=[
            pltpu.VMEM((D, D), BF16), pltpu.VMEM((D, D), BF16), pltpu.VMEM((D, D), BF16), pltpu.VMEM((D, D), BF16),
            pltpu.VMEM((D, FF), BF16), pltpu.VMEM((FF, D), BF16),
            pltpu.VMEM((D, D), BF16),
            pltpu.VMEM((TOK, D), BF16),
            pltpu.VMEM((4, BLK, D), BF16),
            pltpu.VMEM((ROUNDS * TOK, D), BF16),
            pltpu.VMEM((32, BLK, D), BF16),
            pltpu.VMEM((HEADS, 2 * HEAD, TOK), BF16),
            pltpu.VMEM((2 * TOK, D), BF16),
            pltpu.VMEM((HEADS, VROWS, 2 * TOK), BF16),
            pltpu.VMEM((HEADS, VROWS, TOK), F32),
            pltpu.VMEM((HEADS, 1, TOK), F32),
            pltpu.VMEM((2, 8, TOK), F32),
            pltpu.VMEM((2, 2 * TOK, TOK), F32),
            pltpu.VMEM((2, 2 * TOK, TOK), BF16),
            pltpu.VMEM((D, TOK), F32),
            dma((6,)),
            dma, dma((ROUNDS - 1,)),
            dma, dma((3,)), dma, dma,
        ],
        compiler_params=pltpu.CompilerParams(
            collective_id=0, has_side_effects=True, vmem_limit_bytes=60 * 2**20
        ),
        name="layer",
    )(block_len, cross_blocks.T, cross_count, features, w_query, w_key, w_value, w_out, w_up, w_down)


def solution(mesh):
    both = P(("group", "dom"))
    rows = P(("group", "dom"), None)
    return jax.shard_map(
        body,
        mesh=mesh,
        in_specs=(rows, P(), P(), P(), P(), P(), P(), both, rows, both),
        out_specs=rows,
        check_vma=False,
    )
```

```python
import functools
import math

import jax
import jax.numpy as jnp
from jax import lax
from jax.experimental import pallas as pl
from jax.experimental.pallas import tpu as pltpu
from jax.sharding import PartitionSpec as P

F32, BF16 = jnp.float32, jnp.bfloat16
MESH = pl.DeviceIdType.MESH
HEADS = 8
HEAD = 64
BLK = 128
TOK = 512
D = 512
FF = 2048
VROWS = 80
ROUNDS = 16
NEG = -1e30
FLAG = 64.0
SOURCE = (
    (-1, 0), (-1, 2), (-1, 1), (-1, 3), (0, 0), (0, 1), (0, 3), (1, 3),
    (1, 1), (2, 0), (4, 1), (4, 3), (5, 0), (7, 0), (10, 0),
)


def dot(a, b):
    return jnp.dot(a, b, preferred_element_type=F32)


def dot_t(a, b):
    return lax.dot_general(a, b, (((1,), (1,)), ((), ())), preferred_element_type=F32)


def rms(wide):
    return (wide * lax.rsqrt(jnp.mean(wide * wide, axis=-1, keepdims=True) + 1e-06)).astype(BF16)


def kernel(
    len_ref, blocks_ref, count_ref, x_ref, wq_hbm, wk_hbm, wv_hbm, wo_hbm, wup_hbm, wdown_hbm,
    out_ref,
    wq, wk, wv, wo, wup, wdown, wvt, nrm, own, rbuf, xbuf, qt, ks, vt, acc, top, chunk_top, st, ps, mix, w_sem,
    s_sem, r_sem, xs_sem, xr_sem, bs_sem, br_sem,
):
    weights = [(wq_hbm, wq), (wk_hbm, wk), (wv_hbm, wv), (wo_hbm, wo), (wup_hbm, wup), (wdown_hbm, wdown)]

    def fetch(k):
        return pltpu.make_async_copy(weights[k][0], weights[k][1], w_sem.at[k])

    for k in range(3):
        fetch(k).start()

    g, d = lax.axis_index("group"), lax.axis_index("dom")
    y, z = d // 4, d % 4
    up_y, dn_y = (y + 1) % 4 * 4 + z, (y + 3) % 4 * 4 + z
    up_z, dn_z = y * 4 + (z + 1) % 4, y * 4 + (z + 3) % 4
    towards = [(g, up_y), (g, up_z), (g, dn_y), (g, dn_z)]
    up_x, dn_x, sibling = ((g + 2) % 8, d), ((g + 6) % 8, d), (g + 1 - 2 * (g % 2), d)

    barrier = pltpu.get_barrier_semaphore()
    for other in [*towards, up_x, dn_x, sibling]:
        pl.semaphore_signal(barrier, inc=1, device_id=other, device_id_type=MESH)

    normed = rms(x_ref[...].astype(F32))
    nrm[...] = normed
    row = lax.broadcasted_iota(jnp.int32, (BLK, D), 0)
    lane = lax.broadcasted_iota(jnp.int32, (BLK, D), 1)
    flag = jnp.where((lane == 0) | (lane == 64), FLAG, 0.0)
    for b in range(4):
        part = normed[b * BLK:(b + 1) * BLK].astype(F32)
        flagged = jnp.where(row < len_ref[b], part, flag).astype(BF16)
        rbuf[b * BLK:(b + 1) * BLK, :] = flagged
        own[b] = flagged

    pl.semaphore_wait(barrier, 7)

    def whole(ref, sem):
        return pltpu.make_async_remote_copy(
            src_ref=ref, dst_ref=ref, send_sem=sem, recv_sem=sem, device_id=sibling, device_id_type=MESH
        )

    def landed(ref, sem):
        whole(ref, sem).wait_recv()

    def left(ref, sem):
        whole(ref, sem).wait_send()

    def send(n, link):
        arrival, other = SOURCE[n]
        return pltpu.make_async_remote_copy(
            src_ref=rbuf.at[pl.ds((arrival + 1) * TOK + (link ^ other) * BLK, BLK)],
            dst_ref=rbuf.at[pl.ds((n + 1) * TOK + link * BLK, BLK)],
            send_sem=s_sem, recv_sem=r_sem.at[n],
            device_id=towards[link], device_id_type=MESH,
        )

    def start(n):
        if n < ROUNDS - 1:
            for link in range(4):
                send(n, link).start()

    def arrive(n):
        landed(rbuf.at[pl.ds(pl.multiple_of((n + 1) * TOK, TOK), TOK)], r_sem.at[n])

    def send_x(s, way):
        return pltpu.make_async_remote_copy(
            src_ref=own.at[pl.ds(2 * way, 2)] if s == 0 else xbuf.at[pl.ds(4 * s + 2 * way, 2)],
            dst_ref=xbuf.at[pl.ds(4 * s + 4 + 2 * way, 2)],
            send_sem=xs_sem, recv_sem=xr_sem.at[s],
            device_id=(up_x, dn_x)[way], device_id_type=MESH,
        )

    def send_sibling(s):
        return pltpu.make_async_remote_copy(
            src_ref=own if s == 0 else xbuf.at[pl.ds(4 * s, 4)],
            dst_ref=xbuf.at[pl.ds(16 + 4 * s, 4)],
            send_sem=bs_sem, recv_sem=br_sem,
            device_id=sibling, device_id_type=MESH,
        )

    def step_x(s):
        landed(xbuf.at[pl.ds(4 * s, 4)], xr_sem.at[s - 1])
        if s < 3:
            for way in range(2):
                send_x(s, way).start()
        send_sibling(s).start()

    start(0)
    for way in range(2):
        send_x(0, way).start()
    send_sibling(0).start()
    for k in range(3, 6):
        fetch(k).start()

    fetch(0).wait()
    q_all = dot_t(jnp.transpose(wq[...].astype(F32)).astype(BF16), nrm[...]) * (math.log2(math.e) / 8.0)
    q_all = q_all.astype(BF16)
    ones = jnp.ones((HEAD, TOK), BF16)
    for h in range(HEADS):
        at = (h % 2) * HEAD
        qt[h, at:at + HEAD, :] = q_all[h * HEAD:(h + 1) * HEAD]
        qt[h, HEAD - at:HEAD - at + HEAD, :] = ones
        vt[h, HEAD:VROWS, :] = jnp.ones((VROWS - HEAD, 2 * TOK), BF16)
    fetch(1).wait()
    fetch(2).wait()
    wvt[...] = jnp.transpose(wv[...].astype(F32)).astype(BF16)
    acc[...] = jnp.zeros_like(acc)
    top[...] = jnp.full_like(top, NEG)

    def keys_of(rows, unused=None):
        n = rows.shape[0]
        ks[0:n, :] = dot(rows, wk[...]).astype(BF16)
        values = dot_t(wvt[...], rows).astype(BF16)
        for h in range(HEADS):
            vt[h, 0:HEAD, 0:n] = values[h * HEAD:(h + 1) * HEAD]
        mask = jnp.where(rows[:, 0:BLK].astype(F32) > FLAG / 2, NEG, 0.0)
        if unused is not None:
            mask = jnp.where(unused, NEG, mask)
        return mask.astype(BF16)

    def scores(h, at, n, mask, q):
        lane = lax.broadcasted_iota(jnp.int32, (n, BLK), 1)
        pair = ks[at:at + n, (h // 2) * BLK:(h // 2 + 1) * BLK]
        mine = (lane < HEAD) if h % 2 == 0 else (lane >= HEAD)
        return dot(jnp.where(mine, pair, mask[at:at + n]), q)

    def pipeline(units, first, second, third):
        first(0)
        first(1)
        second(0)
        for u in range(units):
            if u + 1 < units:
                second(u + 1)
            if u + 2 < units:
                first(u + 2)
            third(u)

    def attend(rows):
        n = rows.shape[0]
        mask = keys_of(rows)

        def first(h):
            s = scores(h, 0, n, mask, qt[h])
            st[h % 2, 0:n] = s
            chunk_top[h % 2] = jnp.max(s.reshape(n // 8, 8, TOK), axis=0)

        def second(h):
            old = top[h]
            new = jnp.maximum(old, jnp.max(chunk_top[h % 2], axis=0, keepdims=True))
            top[h] = new
            ps[h % 2, 0:n] = jnp.exp2(st[h % 2, 0:n] - new).astype(BF16)
            acc[h] = acc[h] * jnp.exp2(old - new)

        def third(h):
            acc[h] += dot(vt[h, :, 0:n], ps[h % 2, 0:n])

        pipeline(HEADS, first, second, third)

    def cross():
        picked, unused = [], []
        for b in range(4):
            for c in range(2):
                block = blocks_ref[c, b]
                group, local = lax.div(block, 64), lax.rem(block, 4)
                apart = (lax.div(g, 2) - lax.div(group, 2)) * (1 - 2 * lax.div(local, 2))
                slot = lax.rem(group + g, 2) * 16 + lax.rem(apart + 4, 4) * 4 + local
                picked.append(xbuf[slot])
            at = lax.broadcasted_iota(jnp.int32, (2 * BLK, BLK), 0) // BLK
            unused.append(at >= count_ref[b])
        mask = keys_of(jnp.concatenate(picked, axis=0), jnp.concatenate(unused, axis=0))
        n = 2 * BLK

        def first(u):
            h, b = u % HEADS, u // HEADS
            st[u % 2, 0:n, 0:BLK] = scores(h, b * n, n, mask, qt[h, :, b * BLK:(b + 1) * BLK])

        def second(u):
            s = st[u % 2, 0:n, 0:BLK]
            ps[u % 2, 0:n, 0:BLK] = jnp.exp2(s - jnp.max(s, axis=0, keepdims=True)).astype(BF16)

        def third(u):
            h, b = u % HEADS, u // HEADS
            o = dot(vt[h, :, b * n:(b + 1) * n], ps[u % 2, 0:n, 0:BLK])
            mix[h * HEAD:(h + 1) * HEAD, b * BLK:(b + 1) * BLK] = o[0:HEAD] * (1.0 / o[HEAD:HEAD + 1])

        pipeline(4 * HEADS, first, second, third)

    start(1)

    def single(r, carry):
        @pl.when(r == 1)
        def _():
            start(2)
            arrive(0)
            start(3)
            start(4)

        @pl.when(r == 2)
        def _():
            arrive(1)
            start(5)
            start(6)

        attend(rbuf[pl.ds(pl.multiple_of(r * TOK, TOK), TOK), :])
        return carry

    lax.fori_loop(0, 3, single, 0)

    def double(r, carry):
        arrive(2 * r + 2)
        arrive(2 * r + 3)
        for k, sends in ((0, (7, 8, 9)), (1, (10, 11, 12)), (2, (13,)), (4, (14,))):
            @pl.when(r == k)
            def _(k=k, sends=sends):
                for n in sends:
                    start(n)
                if k % 2 == 0:
                    step_x(k // 2 + 1)
        attend(rbuf[pl.ds(pl.multiple_of((2 * r + 3) * TOK, TOK), 2 * TOK), :])
        return carry

    lax.fori_loop(0, 6, double, 0)

    landed(xbuf.at[pl.ds(16, 16)], br_sem)
    cross()
    arrive(ROUNDS - 2)
    attend(rbuf[(ROUNDS - 1) * TOK:ROUNDS * TOK, :])

    left(rbuf.at[pl.ds(0, (ROUNDS - 1) * TOK)], s_sem)
    left(xbuf.at[pl.ds(0, 12)], xs_sem)
    left(xbuf.at[pl.ds(0, 16)], bs_sem)

    for h in range(HEADS):
        at = slice(h * HEAD, (h + 1) * HEAD)
        mix[at, :] = mix[at, :] + acc[h, 0:HEAD] * (1.0 / acc[h, HEAD:HEAD + 1])
    mixed = jnp.transpose(mix[...]).astype(BF16)
    for k in range(3, 6):
        fetch(k).wait()
    resid = (x_ref[...].astype(F32) + dot(mixed, wo[...])).astype(BF16)
    normed_two = rms(resid.astype(F32))
    mix[...] = resid.astype(F32)

    def first(k):
        st[k % 2, 0:TOK] = dot(normed_two, wup[:, k * TOK:(k + 1) * TOK])

    def second(k):
        ps[k % 2, 0:TOK] = jax.nn.gelu(st[k % 2, 0:TOK]).astype(BF16)

    def third(k):
        mix[...] += dot(ps[k % 2, 0:TOK], wdown[k * TOK:(k + 1) * TOK, :])

    pipeline(FF // TOK, first, second, third)
    out_ref[...] = mix[...].astype(out_ref.dtype)


def body(features, w_query, w_key, w_value, w_out, w_up, w_down, block_len, cross_blocks, cross_count):
    smem = pl.BlockSpec(memory_space=pltpu.SMEM)
    vmem = pl.BlockSpec(memory_space=pltpu.VMEM)
    hbm = pl.BlockSpec(memory_space=pl.ANY)
    dma = pltpu.SemaphoreType.DMA
    return pl.pallas_call(
        kernel,
        out_shape=jax.ShapeDtypeStruct((TOK, D), BF16),
        in_specs=[smem] * 3 + [vmem] + [hbm] * 6,
        out_specs=vmem,
        scratch_shapes=[
            pltpu.VMEM((D, D), BF16), pltpu.VMEM((D, D), BF16), pltpu.VMEM((D, D), BF16), pltpu.VMEM((D, D), BF16),
            pltpu.VMEM((D, FF), BF16), pltpu.VMEM((FF, D), BF16),
            pltpu.VMEM((D, D), BF16),
            pltpu.VMEM((TOK, D), BF16),
            pltpu.VMEM((4, BLK, D), BF16),
            pltpu.VMEM((ROUNDS * TOK, D), BF16),
            pltpu.VMEM((32, BLK, D), BF16),
            pltpu.VMEM((HEADS, 2 * HEAD, TOK), BF16),
            pltpu.VMEM((2 * TOK, D), BF16),
            pltpu.VMEM((HEADS, VROWS, 2 * TOK), BF16),
            pltpu.VMEM((HEADS, VROWS, TOK), F32),
            pltpu.VMEM((HEADS, 1, TOK), F32),
            pltpu.VMEM((2, 8, TOK), F32),
            pltpu.VMEM((2, 2 * TOK, TOK), F32),
            pltpu.VMEM((2, 2 * TOK, TOK), BF16),
            pltpu.VMEM((D, TOK), F32),
            dma((6,)),
            dma, dma((ROUNDS - 1,)),
            dma, dma((3,)), dma, dma,
        ],
        compiler_params=pltpu.CompilerParams(
            collective_id=0, has_side_effects=True, vmem_limit_bytes=60 * 2**20
        ),
        name="layer",
    )(block_len, cross_blocks.T, cross_count, features, w_query, w_key, w_value, w_out, w_up, w_down)


def solution(mesh):
    both = P(("group", "dom"))
    rows = P(("group", "dom"), None)
    return jax.shard_map(
        body,
        mesh=mesh,
        in_specs=(rows, P(), P(), P(), P(), P(), P(), both, rows, both),
        out_specs=rows,
        check_vma=False,
    )
```

```python
import functools
import math

import jax
import jax.numpy as jnp
from jax import lax
from jax.experimental import pallas as pl
from jax.experimental.pallas import tpu as pltpu
from jax.sharding import PartitionSpec as P

F32, BF16 = jnp.float32, jnp.bfloat16
MESH = pl.DeviceIdType.MESH
HEADS = 8
HEAD = 64
BLK = 128
TOK = 512
D = 512
FF = 2048
VROWS = 80
ROUNDS = 16
NEG = -1e30
FLAG = 64.0
SOURCE = (
    (-1, 0), (-1, 2), (-1, 1), (-1, 3), (0, 0), (0, 1), (0, 3), (1, 3),
    (1, 1), (2, 0), (4, 1), (4, 3), (5, 0), (7, 0), (10, 0),
)


def dot(a, b):
    return jnp.dot(a, b, preferred_element_type=F32)


def dot_t(a, b):
    return lax.dot_general(a, b, (((1,), (1,)), ((), ())), preferred_element_type=F32)


def rms(wide):
    return (wide * lax.rsqrt(jnp.mean(wide * wide, axis=-1, keepdims=True) + 1e-06)).astype(BF16)


def kernel(
    len_ref, blocks_ref, count_ref, x_ref, wq_hbm, wk_hbm, wv_hbm, wo_hbm, wup_hbm, wdown_hbm,
    out_ref,
    wq, wk, wv, wo, wup, wdown, wvt, nrm, own, rbuf, xbuf, qt, ks, vt, acc, top, chunk_top, st, ps, mix, w_sem,
    s_sem, r_sem, xs_sem, xr_sem, bs_sem, br_sem,
):
    weights = [(wq_hbm, wq), (wk_hbm, wk), (wv_hbm, wv), (wo_hbm, wo), (wup_hbm, wup), (wdown_hbm, wdown)]

    def fetch(k):
        return pltpu.make_async_copy(weights[k][0], weights[k][1], w_sem.at[k])

    for k in range(3):
        fetch(k).start()

    g, d = lax.axis_index("group"), lax.axis_index("dom")
    y, z = d // 4, d % 4
    up_y, dn_y = (y + 1) % 4 * 4 + z, (y + 3) % 4 * 4 + z
    up_z, dn_z = y * 4 + (z + 1) % 4, y * 4 + (z + 3) % 4
    towards = [(g, up_y), (g, up_z), (g, dn_y), (g, dn_z)]
    up_x, dn_x, sibling = ((g + 2) % 8, d), ((g + 6) % 8, d), (g + 1 - 2 * (g % 2), d)

    barrier = pltpu.get_barrier_semaphore()
    for other in [*towards, up_x, dn_x, sibling]:
        pl.semaphore_signal(barrier, inc=1, device_id=other, device_id_type=MESH)

    normed = rms(x_ref[...].astype(F32))
    nrm[...] = normed
    row = lax.broadcasted_iota(jnp.int32, (BLK, D), 0)
    lane = lax.broadcasted_iota(jnp.int32, (BLK, D), 1)
    flag = jnp.where((lane == 0) | (lane == 64), FLAG, 0.0)
    for b in range(4):
        part = normed[b * BLK:(b + 1) * BLK].astype(F32)
        flagged = jnp.where(row < len_ref[b], part, flag).astype(BF16)
        rbuf[b * BLK:(b + 1) * BLK, :] = flagged
        own[b] = flagged

    pl.semaphore_wait(barrier, 7)

    def whole(ref, sem):
        return pltpu.make_async_remote_copy(
            src_ref=ref, dst_ref=ref, send_sem=sem, recv_sem=sem, device_id=sibling, device_id_type=MESH
        )

    def landed(ref, sem):
        whole(ref, sem).wait_recv()

    def left(ref, sem):
        whole(ref, sem).wait_send()

    def send(n, link):
        arrival, other = SOURCE[n]
        return pltpu.make_async_remote_copy(
            src_ref=rbuf.at[pl.ds((arrival + 1) * TOK + (link ^ other) * BLK, BLK)],
            dst_ref=rbuf.at[pl.ds((n + 1) * TOK + link * BLK, BLK)],
            send_sem=s_sem, recv_sem=r_sem.at[n],
            device_id=towards[link], device_id_type=MESH,
        )

    def start(n):
        if n < ROUNDS - 1:
            for link in range(4):
                send(n, link).start()

    def arrive(n):
        landed(rbuf.at[pl.ds(pl.multiple_of((n + 1) * TOK, TOK), TOK)], r_sem.at[n])

    def send_x(s, way):
        return pltpu.make_async_remote_copy(
            src_ref=own.at[pl.ds(2 * way, 2)] if s == 0 else xbuf.at[pl.ds(4 * s + 2 * way, 2)],
            dst_ref=xbuf.at[pl.ds(4 * s + 4 + 2 * way, 2)],
            send_sem=xs_sem, recv_sem=xr_sem.at[s],
            device_id=(up_x, dn_x)[way], device_id_type=MESH,
        )

    def send_sibling(s):
        return pltpu.make_async_remote_copy(
            src_ref=own if s == 0 else xbuf.at[pl.ds(4 * s, 4)],
            dst_ref=xbuf.at[pl.ds(16 + 4 * s, 4)],
            send_sem=bs_sem, recv_sem=br_sem,
            device_id=sibling, device_id_type=MESH,
        )

    def step_x(s):
        landed(xbuf.at[pl.ds(4 * s, 4)], xr_sem.at[s - 1])
        if s < 3:
            for way in range(2):
                send_x(s, way).start()
        send_sibling(s).start()

    start(0)
    for way in range(2):
        send_x(0, way).start()
    send_sibling(0).start()
    for k in range(3, 6):
        fetch(k).start()

    fetch(0).wait()
    q_all = dot_t(jnp.transpose(wq[...].astype(F32)).astype(BF16), nrm[...]) * (math.log2(math.e) / 8.0)
    q_all = q_all.astype(BF16)
    ones = jnp.ones((HEAD, TOK), BF16)
    for h in range(HEADS):
        at = (h % 2) * HEAD
        qt[h, at:at + HEAD, :] = q_all[h * HEAD:(h + 1) * HEAD]
        qt[h, HEAD - at:HEAD - at + HEAD, :] = ones
        vt[h, HEAD:VROWS, :] = jnp.ones((VROWS - HEAD, 2 * TOK), BF16)
    fetch(1).wait()
    fetch(2).wait()
    wvt[...] = jnp.transpose(wv[...].astype(F32)).astype(BF16)
    acc[...] = jnp.zeros_like(acc)
    top[...] = jnp.full_like(top, NEG)

    def keys_of(rows, unused=None):
        n = rows.shape[0]
        ks[0:n, :] = dot(rows, wk[...]).astype(BF16)
        mask = jnp.where(rows[:, 0:BLK].astype(F32) > FLAG / 2, NEG, 0.0)
        if unused is not None:
            mask = jnp.where(unused, NEG, mask)
        return mask.astype(BF16)

    def values_of(rows):
        n = rows.shape[0]
        values = dot_t(wvt[...], rows).astype(BF16)
        for h in range(HEADS):
            vt[h, 0:HEAD, 0:n] = values[h * HEAD:(h + 1) * HEAD]

    def scores(h, at, n, mask, q):
        lane = lax.broadcasted_iota(jnp.int32, (n, BLK), 1)
        pair = ks[at:at + n, (h // 2) * BLK:(h // 2 + 1) * BLK]
        mine = (lane < HEAD) if h % 2 == 0 else (lane >= HEAD)
        return dot(jnp.where(mine, pair, mask[at:at + n]), q)

    def pipeline(units, first, second, third, early=lambda: None):
        first(0)
        first(1)
        early()
        second(0)
        for u in range(units):
            if u + 1 < units:
                second(u + 1)
            if u + 2 < units:
                first(u + 2)
            third(u)

    def attend(rows):
        n = rows.shape[0]
        mask = keys_of(rows)

        def first(h):
            s = scores(h, 0, n, mask, qt[h])
            st[h % 2, 0:n] = s
            chunk_top[h % 2] = jnp.max(s.reshape(n // 8, 8, TOK), axis=0)

        def second(h):
            old = top[h]
            new = jnp.maximum(old, jnp.max(chunk_top[h % 2], axis=0, keepdims=True))
            top[h] = new
            ps[h % 2, 0:n] = jnp.exp2(st[h % 2, 0:n] - new).astype(BF16)
            acc[h] = acc[h] * jnp.exp2(old - new)

        def third(h):
            acc[h] += dot(vt[h, :, 0:n], ps[h % 2, 0:n])

        pipeline(HEADS, first, second, third, lambda: values_of(rows))

    def cross():
        picked, unused = [], []
        for b in range(4):
            for c in range(2):
                block = blocks_ref[c, b]
                group, local = lax.div(block, 64), lax.rem(block, 4)
                apart = (lax.div(g, 2) - lax.div(group, 2)) * (1 - 2 * lax.div(local, 2))
                slot = lax.rem(group + g, 2) * 16 + lax.rem(apart + 4, 4) * 4 + local
                picked.append(xbuf[slot])
            at = lax.broadcasted_iota(jnp.int32, (2 * BLK, BLK), 0) // BLK
            unused.append(at >= count_ref[b])
        rows = jnp.concatenate(picked, axis=0)
        mask = keys_of(rows, jnp.concatenate(unused, axis=0))
        n = 2 * BLK

        def first(u):
            h, b = u % HEADS, u // HEADS
            st[u % 2, 0:n, 0:BLK] = scores(h, b * n, n, mask, qt[h, :, b * BLK:(b + 1) * BLK])

        def second(u):
            s = st[u % 2, 0:n, 0:BLK]
            ps[u % 2, 0:n, 0:BLK] = jnp.exp2(s - jnp.max(s, axis=0, keepdims=True)).astype(BF16)

        def third(u):
            h, b = u % HEADS, u // HEADS
            o = dot(vt[h, :, b * n:(b + 1) * n], ps[u % 2, 0:n, 0:BLK])
            mix[h * HEAD:(h + 1) * HEAD, b * BLK:(b + 1) * BLK] = o[0:HEAD] * (1.0 / o[HEAD:HEAD + 1])

        pipeline(4 * HEADS, first, second, third, lambda: values_of(rows))

    start(1)

    def single(r, carry):
        @pl.when(r == 1)
        def _():
            start(2)
            arrive(0)
            start(3)
            start(4)

        @pl.when(r == 2)
        def _():
            arrive(1)
            start(5)
            start(6)

        attend(rbuf[pl.ds(pl.multiple_of(r * TOK, TOK), TOK), :])
        return carry

    lax.fori_loop(0, 3, single, 0)

    def double(r, carry):
        arrive(2 * r + 2)
        arrive(2 * r + 3)
        for k, sends in ((0, (7, 8, 9)), (1, (10, 11, 12)), (2, (13,)), (4, (14,))):
            @pl.when(r == k)
            def _(k=k, sends=sends):
                for n in sends:
                    start(n)
                if k % 2 == 0:
                    step_x(k // 2 + 1)
        attend(rbuf[pl.ds(pl.multiple_of((2 * r + 3) * TOK, TOK), 2 * TOK), :])
        return carry

    lax.fori_loop(0, 6, double, 0)

    landed(xbuf.at[pl.ds(16, 16)], br_sem)
    cross()
    arrive(ROUNDS - 2)
    attend(rbuf[(ROUNDS - 1) * TOK:ROUNDS * TOK, :])

    left(rbuf.at[pl.ds(0, (ROUNDS - 1) * TOK)], s_sem)
    left(xbuf.at[pl.ds(0, 12)], xs_sem)
    left(xbuf.at[pl.ds(0, 16)], bs_sem)

    for h in range(HEADS):
        at = slice(h * HEAD, (h + 1) * HEAD)
        mix[at, :] = mix[at, :] + acc[h, 0:HEAD] * (1.0 / acc[h, HEAD:HEAD + 1])
    mixed = jnp.transpose(mix[...]).astype(BF16)
    for k in range(3, 6):
        fetch(k).wait()
    resid = (x_ref[...].astype(F32) + dot(mixed, wo[...])).astype(BF16)
    normed_two = rms(resid.astype(F32))
    mix[...] = resid.astype(F32)

    def first(k):
        st[k % 2, 0:TOK] = dot(normed_two, wup[:, k * TOK:(k + 1) * TOK])

    def second(k):
        ps[k % 2, 0:TOK] = jax.nn.gelu(st[k % 2, 0:TOK]).astype(BF16)

    def third(k):
        mix[...] += dot(ps[k % 2, 0:TOK], wdown[k * TOK:(k + 1) * TOK, :])

    pipeline(FF // TOK, first, second, third)
    out_ref[...] = mix[...].astype(out_ref.dtype)


def body(features, w_query, w_key, w_value, w_out, w_up, w_down, block_len, cross_blocks, cross_count):
    smem = pl.BlockSpec(memory_space=pltpu.SMEM)
    vmem = pl.BlockSpec(memory_space=pltpu.VMEM)
    hbm = pl.BlockSpec(memory_space=pl.ANY)
    dma = pltpu.SemaphoreType.DMA
    return pl.pallas_call(
        kernel,
        out_shape=jax.ShapeDtypeStruct((TOK, D), BF16),
        in_specs=[smem] * 3 + [vmem] + [hbm] * 6,
        out_specs=vmem,
        scratch_shapes=[
            pltpu.VMEM((D, D), BF16), pltpu.VMEM((D, D), BF16), pltpu.VMEM((D, D), BF16), pltpu.VMEM((D, D), BF16),
            pltpu.VMEM((D, FF), BF16), pltpu.VMEM((FF, D), BF16),
            pltpu.VMEM((D, D), BF16),
            pltpu.VMEM((TOK, D), BF16),
            pltpu.VMEM((4, BLK, D), BF16),
            pltpu.VMEM((ROUNDS * TOK, D), BF16),
            pltpu.VMEM((32, BLK, D), BF16),
            pltpu.VMEM((HEADS, 2 * HEAD, TOK), BF16),
            pltpu.VMEM((2 * TOK, D), BF16),
            pltpu.VMEM((HEADS, VROWS, 2 * TOK), BF16),
            pltpu.VMEM((HEADS, VROWS, TOK), F32),
            pltpu.VMEM((HEADS, 1, TOK), F32),
            pltpu.VMEM((2, 8, TOK), F32),
            pltpu.VMEM((2, 2 * TOK, TOK), F32),
            pltpu.VMEM((2, 2 * TOK, TOK), BF16),
            pltpu.VMEM((D, TOK), F32),
            dma((6,)),
            dma, dma((ROUNDS - 1,)),
            dma, dma((3,)), dma, dma,
        ],
        compiler_params=pltpu.CompilerParams(
            collective_id=0, has_side_effects=True, vmem_limit_bytes=60 * 2**20
        ),
        name="layer",
    )(block_len, cross_blocks.T, cross_count, features, w_query, w_key, w_value, w_out, w_up, w_down)


def solution(mesh):
    both = P(("group", "dom"))
    rows = P(("group", "dom"), None)
    return jax.shard_map(
        body,
        mesh=mesh,
        in_specs=(rows, P(), P(), P(), P(), P(), P(), both, rows, both),
        out_specs=rows,
        check_vma=False,
    )
```
